32 devices in a mesh: dp: 16 (over z, y, x), tensor: 2 (over core).
Axes of the slice: x: 2, y: 2, z: 4, core: 2. Of those that a mesh axis runs over, the one named last changes fastest.
Arguments:
- tokens: bfloat16 [32768, 640], P(('dp', 'tensor')), may hold values from -6 to 6
- w_query: bfloat16 [640, 1024], P('dp', 'tensor'), may hold values from -0.25 to 0.25
- w_key: bfloat16 [640, 256], P('dp'), may hold values from -0.25 to 0.25
- w_value: bfloat16 [640, 256], P('dp'), may hold values from -0.25 to 0.25
- w_out: bfloat16 [1024, 640], P('tensor', 'dp'), may hold values from -0.1875 to 0.1875
- gain_attn: bfloat16 [640], P('dp'), may hold values from 0.5 to 1.5
- gain_query: bfloat16 [256], P('dp'), may hold values from 0.5 to 1.5
- gain_key: bfloat16 [256], P('dp'), may hold values from 0.5 to 1.5
- gain_post_attn: bfloat16 [640], P('dp'), may hold values from 0.5 to 1.5
- w_gate: bfloat16 [640, 2048], P('dp', 'tensor'), may hold values from -0.25 to 0.25
- w_up: bfloat16 [640, 2048], P('dp', 'tensor'), may hold values from -0.25 to 0.25
- w_down: bfloat16 [2048, 640], P('tensor', 'dp'), may hold values from -0.125 to 0.125
- gain_pre_ffn: bfloat16 [640], P('dp'), may hold values from 0.5 to 1.5
- gain_post_ffn: bfloat16 [640], P('dp'), may hold values from 0.5 to 1.5
- cotangent: bfloat16 [32768, 640], P(('dp', 'tensor')), may hold values from -6 to 6
Outputs:
- output: bfloat16 [32768, 640], P(('dp', 'tensor'))
- tokens_grad: float32 [32768, 640], P(('dp', 'tensor'))
- w_query_grad: float32 [640, 1024], P('dp', 'tensor')
- w_key_grad: float32 [640, 256], P('dp')
- w_value_grad: float32 [640, 256], P('dp')
- w_out_grad: float32 [1024, 640], P('tensor', 'dp')
- gain_attn_grad: float32 [640], P('dp')
- gain_query_grad: float32 [256], P('dp')
- gain_key_grad: float32 [256], P('dp')
- gain_post_attn_grad: float32 [640], P('dp')
- w_gate_grad: float32 [640, 2048], P('dp', 'tensor')
- w_up_grad: float32 [640, 2048], P('dp', 'tensor')
- w_down_grad: float32 [2048, 640], P('tensor', 'dp')
- gain_pre_ffn_grad: float32 [640], P('dp')
- gain_post_ffn_grad: float32 [640], P('dp')
The draws below stay inside these ranges and needn't reach their ends.
All inputs are finite; a program needn't handle non-finite values.
Results may differ from the reference program's by a relative error of at most 0.018.
Values may be sent and summed in bfloat16 or wider, within the bound.
A program may use at most 192 MiB of HBM per device.

```python
import math
import jax
import jax.numpy as jnp
from jax import lax

D = 640
HEADS = 4
HD = 256
FF = 2048
LENGTH = 2048
TOKENS = 32768


def levels(rng, dims, pieces, low, high):
    level, own = 1.0, jax.random.fold_in(rng, 6)
    for position, blocks in pieces:
        heights = jnp.exp(jax.random.uniform(jax.random.fold_in(own, position), (blocks,), jnp.float32, low / len(pieces), high / len(pieces)))
        level = level * jnp.repeat(heights, dims[position] // blocks).reshape([-1 if axis == position else 1 for axis in range(len(dims))])
    return level


def gaussian(stream_key, dims, spread, most, shards=(), kind=jnp.bfloat16):
    loudness = levels(stream_key, dims, shards, -0.22, 0.18) if shards else 1.0
    drawn = jax.random.normal(stream_key, dims, jnp.float32) * spread * loudness
    return jnp.minimum(jnp.maximum(drawn, -most), most).astype(kind)


def setup_inputs(seed: int = 0) -> dict:
    arg_keys = jax.random.split(jax.random.key(seed), 16)
    return {
        "tokens": gaussian(arg_keys[0], (TOKENS, D), 1.0, 6.0, ((0, 32),)),
        "w_query": gaussian(arg_keys[1], (D, HEADS * HD), D ** -0.5, 0.25, ((0, 16), (1, 2))),
        "w_key": gaussian(arg_keys[2], (D, HD), D ** -0.5, 0.25, ((0, 16),)),
        "w_value": gaussian(arg_keys[3], (D, HD), D ** -0.5, 0.25, ((0, 16),)),
        "w_out": gaussian(arg_keys[4], (HEADS * HD, D), (HEADS * HD) ** -0.5, 0.1875, ((0, 2), (1, 16))),
        "gain_attn": jnp.clip(1.0 + 0.1 * jax.random.normal(arg_keys[5], (D,), jnp.float32), 0.5, 1.5).astype(jnp.bfloat16),
        "gain_query": jnp.clip(1.0 + 0.1 * jax.random.normal(arg_keys[6], (HD,), jnp.float32), 0.5, 1.5).astype(jnp.bfloat16),
        "gain_key": jnp.clip(1.0 + 0.1 * jax.random.normal(arg_keys[7], (HD,), jnp.float32), 0.5, 1.5).astype(jnp.bfloat16),
        "gain_post_attn": jnp.clip(1.0 + 0.1 * jax.random.normal(arg_keys[8], (D,), jnp.float32), 0.5, 1.5).astype(jnp.bfloat16),
        "w_gate": gaussian(arg_keys[9], (D, FF), D ** -0.5, 0.25, ((0, 16), (1, 2))),
        "w_up": gaussian(arg_keys[10], (D, FF), D ** -0.5, 0.25, ((0, 16), (1, 2))),
        "w_down": gaussian(arg_keys[11], (FF, D), FF ** -0.5, 0.125, ((0, 2), (1, 16))),
        "gain_pre_ffn": jnp.clip(1.0 + 0.1 * jax.random.normal(arg_keys[12], (D,), jnp.float32), 0.5, 1.5).astype(jnp.bfloat16),
        "gain_post_ffn": jnp.clip(1.0 + 0.1 * jax.random.normal(arg_keys[13], (D,), jnp.float32), 0.5, 1.5).astype(jnp.bfloat16),
        "cotangent": gaussian(arg_keys[14], (TOKENS, D), 1.0, 6.0, ((0, 32),)),
    }


EPS = 1e-06
MASKED = -1e+30
HIGH = lax.Precision.HIGHEST

@jax.custom_vjp
def low(v):
    return lax.optimization_barrier(v.astype(jnp.bfloat16)).astype(jnp.float32)

@jax.custom_vjp
def low_back(v):
    return v

def low_keep(v):
    return (low(v), None)

def low_pass(kept, grad):
    return (grad,)

def back_keep(v):
    return (v, None)

def back_low(kept, grad):
    return (low(grad),)
low.defvjp(low_keep, low_pass)
low_back.defvjp(back_keep, back_low)

def matmul(left, right):
    return jnp.dot(left, right, precision=HIGH, preferred_element_type=jnp.float32)

def norm_rows(value, gain):
    return value * lax.rsqrt(lax.optimization_barrier(jnp.mean(value * value, axis=-1, keepdims=True)) + EPS) * gain

def tables(positions, width):
    half = width // 2
    freqs = jnp.exp(jnp.arange(half, dtype=jnp.float32) * (-2.0 * math.log(1000000.0) / width))
    angles = positions.astype(jnp.float32)[:, None] * freqs[None, :]
    angles = jnp.concatenate([angles, angles], axis=1)
    return (jnp.cos(angles), jnp.sin(angles))

def turn(value, cosine, sine):
    half = value.shape[-1] // 2
    rotated = jnp.concatenate([-value[..., half:], value[..., :half]], axis=-1)
    return value * cosine + rotated * sine

def gelu_tanh(value):
    return jax.nn.gelu(value, approximate=True)

def attend(parts, cosine, sine):
    query, key, value = parts
    query = low(turn(query, cosine[:, None, :], sine[:, None, :]))
    key = low(turn(key, cosine, sine))
    scores = jnp.einsum('qhd,kd->hqk', query, key, precision=HIGH) * HD ** (-0.5)
    places = jnp.arange(LENGTH, dtype=jnp.int32)
    allowed = places[:, None] >= places[None, :]
    scores = low_back(jnp.where(allowed[None], scores, MASKED))
    peak = lax.optimization_barrier(jnp.max(scores, axis=-1, keepdims=True))
    expon = jnp.exp(scores - peak)
    prob = low(expon / lax.optimization_barrier(jnp.sum(expon, axis=-1, keepdims=True)))
    return jnp.einsum('hqk,kd->qhd', prob, value, precision=HIGH)

def layer(inputs, w_query, w_key, w_value, w_out, gain_attn, gain_query, gain_key, gain_post_attn, w_gate, w_up, w_down, gain_pre_ffn, gain_post_ffn):
    count = TOKENS // LENGTH
    cosine, sine = tables(jnp.arange(LENGTH, dtype=jnp.int32), HD)
    normed = low(norm_rows(inputs, gain_attn))
    query_pre = low_back(matmul(normed, w_query)).reshape(TOKENS, HEADS, HD)
    key_pre = low_back(matmul(normed, w_key))
    values = low(low_back(matmul(normed, w_value)))
    query_normed = norm_rows(query_pre, gain_query)
    key_normed = norm_rows(key_pre, gain_key)
    mixed = lax.map(jax.checkpoint(lambda parts: attend(parts, cosine, sine)), (query_normed.reshape(count, LENGTH, HEADS, HD), key_normed.reshape(count, LENGTH, HD), values.reshape(count, LENGTH, HD)))
    mixed = low(low_back(mixed.reshape(TOKENS, HEADS * HD)))
    attn_sum = low_back(matmul(mixed, w_out))
    middle = inputs + norm_rows(attn_sum, gain_post_attn)
    ffn_in = low(norm_rows(middle, gain_pre_ffn))
    gate = low_back(matmul(ffn_in, w_gate))
    up = low_back(matmul(ffn_in, w_up))
    hidden = low(gelu_tanh(gate) * up)
    ffn_sum = low_back(matmul(hidden, w_down))
    return middle + norm_rows(ffn_sum, gain_post_ffn)

def reference(tokens, w_query, w_key, w_value, w_out, gain_attn, gain_query, gain_key, gain_post_attn, w_gate, w_up, w_down, gain_pre_ffn, gain_post_ffn, cotangent):
    floats = [a.astype(jnp.float32) for a in (tokens, w_query, w_key, w_value, w_out, gain_attn, gain_query, gain_key, gain_post_attn, w_gate, w_up, w_down, gain_pre_ffn, gain_post_ffn)]
    result, pull = jax.vjp(layer, *floats)
    grads = pull(cotangent.astype(jnp.float32))
    return (result.astype(jnp.bfloat16), grads[0], grads[1], grads[2], grads[3], grads[4], grads[5], grads[6], grads[7], grads[8], grads[9], grads[10], grads[11], grads[12], grads[13])
```

```python
import functools
import math

import jax
import jax.numpy as jnp
from jax import lax
from jax.experimental import pallas as pl
from jax.experimental.pallas import tpu as pltpu
from jax.sharding import PartitionSpec as P

EPS = 1e-06
MASKED = -1e30


def matmul(left, right):
    return jnp.dot(left, right, preferred_element_type=jnp.float32)


def times_transposed(left, right):
    return lax.dot_general(
        left, right, (((1,), (1,)), ((), ())), preferred_element_type=jnp.float32
    )


def transposed_times(left, right):
    return lax.dot_general(
        left, right, (((0,), (0,)), ((), ())), preferred_element_type=jnp.float32
    )


def norm_rows(value, gain):
    scale = lax.rsqrt(jnp.mean(value * value, axis=-1, keepdims=True) + EPS)
    unit = value * scale
    return (unit * gain, unit, scale)


def norm_back(grad, unit, scale, gain, axes):
    gain_grad = jnp.sum(grad * unit, axis=axes)
    inner = grad * gain
    return (scale * (inner - unit * jnp.mean(inner * unit, axis=-1, keepdims=True)), gain_grad)


def tables(length, width, inner=64):
    half = width // 2
    freqs = jnp.exp(jnp.arange(half, dtype=jnp.float32) * (-2.0 * math.log(1000000.0) / width))
    coarse = (jnp.arange(length // inner, dtype=jnp.float32) * inner)[:, None] * freqs
    fine = jnp.arange(inner, dtype=jnp.float32)[:, None] * freqs
    cos_a, sin_a = jnp.cos(coarse)[:, None], jnp.sin(coarse)[:, None]
    cos_b, sin_b = jnp.cos(fine)[None], jnp.sin(fine)[None]
    cosine = (cos_a * cos_b - sin_a * sin_b).reshape(length, half)
    sine = (sin_a * cos_b + cos_a * sin_b).reshape(length, half)
    return cosine, sine


def turn(value, cosine, sine):
    half = value.shape[-1] // 2
    first, second = value[:, :half], value[:, half:]
    return jnp.concatenate(
        [first * cosine - second * sine, second * cosine + first * sine], axis=-1
    )


def turn_back(grad, cosine, sine):
    half = grad.shape[-1] // 2
    first, second = grad[:, :half], grad[:, half:]
    return jnp.concatenate(
        [first * cosine + second * sine, second * cosine - first * sine], axis=-1
    )


def gelu_tanh(value):
    return jax.nn.gelu(value, approximate=True)


BLOCK = 512
VMEM = 56 * 1024 * 1024


def allowed_keys(size):
    keys = lax.broadcasted_iota(jnp.int32, (size, size), 0)
    queries = lax.broadcasted_iota(jnp.int32, (size, size), 1)
    return queries >= keys


def attend_kernel(heads, width, factor, q_ref, k_ref, vt_ref, o_ref, lse_ref, acc, peak, total):
    block = q_ref.shape[0]
    number = pl.program_id(0)
    queries = [q_ref[:, h * width : (h + 1) * width] * jnp.bfloat16(factor) for h in range(heads)]

    def tile(j, first):
        start = pl.multiple_of(j * block, block)
        keys = k_ref[pl.ds(start, block), :]
        values = vt_ref[:, pl.ds(start, block)]
        for h in range(heads):
            scores = times_transposed(keys, queries[h])
            if first:
                scores = jnp.where(allowed_keys(block), scores, MASKED)
                top = jnp.max(scores, axis=0, keepdims=True)
                expon = jnp.exp(scores - top)
                total[h] = jnp.sum(expon, axis=0, keepdims=True)
                acc[h] = matmul(values, expon.astype(jnp.bfloat16))
            else:
                old = peak[h]
                top = jnp.maximum(old, jnp.max(scores, axis=0, keepdims=True))
                expon = jnp.exp(scores - top)
                scale = jnp.exp(old - top)
                total[h] = total[h] * scale + jnp.sum(expon, axis=0, keepdims=True)
                acc[h] = acc[h] * scale + matmul(values, expon.astype(jnp.bfloat16))
            peak[h] = top

    tile(number, True)

    @pl.loop(0, number)
    def _(j):
        tile(j, False)

    for h in range(heads):
        mixed = acc[h] * (1.0 / total[h])
        o_ref[:, h * width : (h + 1) * width] = mixed.T.astype(jnp.bfloat16)
        lse_ref[h] = peak[h] + jnp.log(total[h])


def attend(query, key, value_t, heads):
    length, width = key.shape
    block = min(BLOCK, length)
    return pl.pallas_call(
        functools.partial(attend_kernel, heads, width, width ** (-0.5)),
        grid=(length // block,),
        in_specs=[
            pl.BlockSpec((block, heads * width), lambda i: (i, 0)),
            pl.BlockSpec((length, width), lambda i: (0, 0)),
            pl.BlockSpec((width, length), lambda i: (0, 0)),
        ],
        out_specs=[
            pl.BlockSpec((block, heads * width), lambda i: (i, 0)),
            pl.BlockSpec((heads, 1, block), lambda i: (0, 0, i)),
        ],
        out_shape=[
            jax.ShapeDtypeStruct((length, heads * width), jnp.bfloat16),
            jax.ShapeDtypeStruct((heads, 1, length), jnp.float32),
        ],
        scratch_shapes=[
            pltpu.VMEM((heads, width, block), jnp.float32),
            pltpu.VMEM((heads, 1, block), jnp.float32),
            pltpu.VMEM((heads, 1, block), jnp.float32),
        ],
        compiler_params=pltpu.CompilerParams(vmem_limit_bytes=VMEM),
        cost_estimate=pl.CostEstimate(
            flops=4 * heads * length * length * width,
            bytes_accessed=8 * length * heads * width,
            transcendentals=heads * length * length,
        ),
        name="attend",
    )(query, key, value_t)


def attend_back_kernel(
    heads, width, factor, q_ref, g_ref, o_ref, lse_ref, k_ref, kt_ref, v_ref,
    dq_ref, dk_ref, dv_ref, dqt, delta,
):
    block = q_ref.shape[0]
    number = pl.program_id(0)
    cols = [slice(h * width, (h + 1) * width) for h in range(heads)]
    queries = [q_ref[:, c] * jnp.bfloat16(factor) for c in cols]

    @pl.when(number == 0)
    def _():
        dk_ref[...] = jnp.zeros_like(dk_ref)
        dv_ref[...] = jnp.zeros_like(dv_ref)

    for h in range(heads):
        product = g_ref[:, cols[h]].astype(jnp.float32) * o_ref[:, cols[h]].astype(jnp.float32)
        delta[h] = jnp.sum(product.T, axis=0, keepdims=True)

    def tile(j, first):
        start = pl.multiple_of(j * block, block)
        rows = pl.ds(start, block)
        keys = k_ref[rows, :]
        keys_t = kt_ref[:, rows]
        values = v_ref[rows, :]
        key_grad = value_grad = None
        for h in range(heads):
            grads = g_ref[:, cols[h]]
            scores = times_transposed(keys, queries[h])
            prob = jnp.exp(scores - lse_ref[h])
            if first:
                prob = jnp.where(allowed_keys(block), prob, 0.0)
            prob_grad = times_transposed(values, grads)
            score_grad = (prob * (prob_grad - delta[h])).astype(jnp.bfloat16)
            more_value = matmul(prob.astype(jnp.bfloat16), grads)
            more_key = matmul(score_grad, queries[h])
            value_grad = more_value if value_grad is None else value_grad + more_value
            key_grad = more_key if key_grad is None else key_grad + more_key
            if first:
                dqt[h] = matmul(keys_t, score_grad)
            else:
                dqt[h] += matmul(keys_t, score_grad)
        dk_ref[rows, :] += key_grad
        dv_ref[rows, :] += value_grad

    tile(number, True)

    @pl.loop(0, number)
    def _(j):
        tile(j, False)

    for h in range(heads):
        dq_ref[:, cols[h]] = dqt[h].T * factor


def attend_back(query, grad, mixed, lse, key, key_t, value, heads):
    length, width = key.shape
    block = min(BLOCK, length)
    rows = pl.BlockSpec((block, heads * width), lambda i: (i, 0))
    whole = pl.BlockSpec((length, width), lambda i: (0, 0))
    return pl.pallas_call(
        functools.partial(attend_back_kernel, heads, width, width ** (-0.5)),
        grid=(length // block,),
        in_specs=[
            rows,
            rows,
            rows,
            pl.BlockSpec((heads, 1, block), lambda i: (0, 0, i)),
            whole,
            pl.BlockSpec((width, length), lambda i: (0, 0)),
            whole,
        ],
        out_specs=[rows, whole, whole],
        out_shape=[
            jax.ShapeDtypeStruct((length, heads * width), jnp.float32),
            jax.ShapeDtypeStruct((length, width), jnp.float32),
            jax.ShapeDtypeStruct((length, width), jnp.float32),
        ],
        scratch_shapes=[
            pltpu.VMEM((heads, width, block), jnp.float32),
            pltpu.VMEM((heads, 1, block), jnp.float32),
        ],
        compiler_params=pltpu.CompilerParams(vmem_limit_bytes=VMEM),
        cost_estimate=pl.CostEstimate(
            flops=10 * heads * length * length * width,
            bytes_accessed=12 * length * heads * width,
            transcendentals=heads * length * length,
        ),
        name="attend_back",
    )(query, grad, mixed, lse, key, key_t, value)


def per_device(
    tokens,
    w_query,
    w_key,
    w_value,
    w_out,
    gain_attn,
    gain_query,
    gain_key,
    gain_post_attn,
    w_gate,
    w_up,
    w_down,
    gain_pre_ffn,
    gain_post_ffn,
    cotangent,
):
    parts = lax.axis_size("tensor")
    spread = lax.axis_size("dp")
    own_rows = tokens.shape[0]
    length = own_rows * parts
    head_dim = w_key.shape[1]
    model = w_query.shape[0] * spread
    share = w_query.shape[0]
    small = gain_query.shape[0]
    heads = w_query.shape[1] // head_dim
    offset = lax.axis_index("tensor") * own_rows
    swap = [(i, (i + 1) % parts) for i in range(parts)]

    def whole_sequence(rows):
        pieces = [rows]
        for _ in range(parts - 1):
            pieces.append(lax.ppermute(pieces[-1], "tensor", swap))
        if parts == 1:
            return rows
        first = lax.axis_index("tensor") == 0
        return jnp.concatenate(
            [jnp.where(first, pieces[0], pieces[1]), jnp.where(first, pieces[1], pieces[0])], axis=0
        )

    def summed(partial):
        low = partial.astype(jnp.bfloat16)
        return low.astype(jnp.float32) + lax.ppermute(low, "tensor", swap).astype(jnp.float32)

    def own(rows):
        return lax.dynamic_slice_in_dim(rows, offset, own_rows, 0)

    def tall(column):
        return jnp.pad(column, (0, share - small))

    gain_block = jnp.stack(
        [gain_attn, gain_post_attn, gain_pre_ffn, gain_post_ffn, tall(gain_query), tall(gain_key)],
        axis=1,
    )
    gain_block = jnp.pad(gain_block, ((0, 0), (0, 128 - gain_block.shape[1])))
    attn_pack = jnp.concatenate([w_query, w_key, w_value, w_out.T, gain_block], axis=1)
    ffn_pack = jnp.concatenate([w_gate, w_up, w_down.T], axis=1)
    attn_all = lax.all_gather(attn_pack, "dp", axis=0, tiled=True)
    attn_all, ffn_pack = lax.optimization_barrier((attn_all, ffn_pack))
    ffn_all = lax.all_gather(ffn_pack, "dp", axis=0, tiled=True)
    low_tokens = whole_sequence(tokens)
    inputs = low_tokens.astype(jnp.float32)
    out_grad = whole_sequence(cotangent).astype(jnp.float32)

    q_cols = heads * head_dim
    places = [0, q_cols, q_cols + head_dim, q_cols + 2 * head_dim, 2 * q_cols + 2 * head_dim]
    query_w, key_w, value_w, out_wt = (
        attn_all[:, places[n] : places[n + 1]] for n in range(4)
    )
    gains = attn_all[:, places[4] :].astype(jnp.float32)
    attn_g, post_attn_g, pre_ffn_g, post_ffn_g = (gains[:, n] for n in range(4))
    query_g, key_g = (
        gains[:, n].reshape(spread, share)[:, :small].reshape(spread * small) for n in (4, 5)
    )
    hidden_units = w_gate.shape[1]
    gate_w, up_w, down_wt = (
        ffn_all[:, n * hidden_units : (n + 1) * hidden_units] for n in range(3)
    )
    cosine, sine = tables(length, head_dim)

    normed, attn_unit, attn_scale = norm_rows(inputs, attn_g)
    normed_low = normed.astype(jnp.bfloat16)
    key_pre = matmul(normed_low, key_w)
    value_low = matmul(normed_low, value_w).astype(jnp.bfloat16)
    key_normed, key_unit, key_scale = norm_rows(key_pre, key_g)
    key_low = turn(key_normed, cosine, sine).astype(jnp.bfloat16)
    query_pre = matmul(normed_low, query_w)
    query_units, query_scales, query_lows = [], [], []
    for h in range(heads):
        normal, unit, scale = norm_rows(query_pre[:, h * head_dim : (h + 1) * head_dim], query_g)
        query_units.append(unit)
        query_scales.append(scale)
        query_lows.append(turn(normal, cosine, sine).astype(jnp.bfloat16))
    query_low = jnp.concatenate(query_lows, axis=1)
    mixed, lse = attend(query_low, key_low, value_low.T, heads)

    attn_sum = summed(times_transposed(mixed, out_wt))
    attn_branch, post_attn_unit, post_attn_scale = norm_rows(attn_sum, post_attn_g)
    middle = inputs + attn_branch
    ffn_normed, pre_ffn_unit, pre_ffn_scale = norm_rows(middle, pre_ffn_g)
    ffn_low = ffn_normed.astype(jnp.bfloat16)
    gate = matmul(ffn_low, gate_w)
    up = matmul(ffn_low, up_w)
    activated, gelu_pull = jax.vjp(gelu_tanh, gate)
    hidden = (activated * up).astype(jnp.bfloat16)
    ffn_sum = summed(times_transposed(hidden, down_wt))
    ffn_branch, post_ffn_unit, post_ffn_scale = norm_rows(ffn_sum, post_ffn_g)
    output = own((middle + ffn_branch).astype(jnp.bfloat16))

    ffn_sum_grad, post_ffn_gain_grad = norm_back(
        out_grad, post_ffn_unit, post_ffn_scale, post_ffn_g, 0
    )
    ffn_sum_low = ffn_sum_grad.astype(jnp.bfloat16)
    hidden_grad = matmul(ffn_sum_low, down_wt)
    gate_grad = gelu_pull(hidden_grad * up)[0].astype(jnp.bfloat16)
    up_grad = (hidden_grad * activated).astype(jnp.bfloat16)
    ffn_in_part = times_transposed(gate_grad, gate_w) + times_transposed(up_grad, up_w)
    ffn_in_grad = summed(ffn_in_part)
    ffn_grads = jnp.concatenate(
        [
            transposed_times(ffn_low, gate_grad),
            transposed_times(ffn_low, up_grad),
            transposed_times(ffn_sum_low, hidden),
        ],
        axis=1,
    )
    middle_part, pre_ffn_gain_grad = norm_back(
        ffn_in_grad, pre_ffn_unit, pre_ffn_scale, pre_ffn_g, 0
    )
    middle_grad = out_grad + middle_part
    attn_sum_grad, post_attn_gain_grad = norm_back(
        middle_grad, post_attn_unit, post_attn_scale, post_attn_g, 0
    )
    attn_sum_low = attn_sum_grad.astype(jnp.bfloat16)
    ffn_grads, attn_sum_low = lax.optimization_barrier((ffn_grads, attn_sum_low))
    ffn_owned = lax.psum_scatter(ffn_grads, "dp", scatter_dimension=0, tiled=True)

    mixed_grad = matmul(attn_sum_low, out_wt).astype(jnp.bfloat16)
    out_wt_grad = transposed_times(attn_sum_low, mixed)
    query_grad, key_grad, value_grad = attend_back(
        query_low, mixed_grad, mixed, lse, key_low, key_low.T, value_low, heads
    )
    query_gain_grad = 0.0
    query_pre_grads = []
    for h in range(heads):
        turned = turn_back(query_grad[:, h * head_dim : (h + 1) * head_dim], cosine, sine)
        pre_grad, gain_grad = norm_back(turned, query_units[h], query_scales[h], query_g, 0)
        query_pre_grads.append(pre_grad.astype(jnp.bfloat16))
        query_gain_grad = query_gain_grad + gain_grad
    key_turned = turn_back(key_grad, cosine, sine)
    key_pre_grad, key_gain_grad = norm_back(key_turned, key_unit, key_scale, key_g, 0)
    joint_grad = jnp.concatenate(
        query_pre_grads + [key_pre_grad.astype(jnp.bfloat16), value_grad.astype(jnp.bfloat16)],
        axis=1,
    )
    normed_part = times_transposed(joint_grad, attn_all[:, : places[3]])
    joint_w_grad = transposed_times(normed_low, joint_grad)
    attn_gain_grad = jnp.sum(normed_part * attn_unit, axis=0)

    def wide(column):
        return jnp.pad(column.reshape(spread, small), ((0, 0), (0, share - small))).reshape(model)

    once = 1.0 / parts
    gain_grads = jnp.stack(
        [
            attn_gain_grad,
            post_attn_gain_grad * once,
            pre_ffn_gain_grad * once,
            post_ffn_gain_grad * once,
            wide(query_gain_grad),
            wide(key_gain_grad),
        ],
        axis=1,
    )
    gain_grads = jnp.pad(gain_grads, ((0, 0), (0, 512 - gain_grads.shape[1])))
    attn_owned = lax.psum_scatter(
        jnp.concatenate([joint_w_grad, out_wt_grad, gain_grads], axis=1),
        "dp",
        scatter_dimension=0,
        tiled=True,
    )
    normed_low_part = normed_part.astype(jnp.bfloat16)
    theirs = lax.dynamic_slice_in_dim(
        normed_low_part, (length - own_rows) - offset, own_rows, 0
    )
    normed_grad = own(normed_part) + lax.ppermute(theirs, "tensor", swap).astype(jnp.float32)
    input_part, _ = norm_back(normed_grad, own(attn_unit), own(attn_scale), attn_g, 0)
    tokens_grad = own(middle_grad) + input_part

    shared = lax.psum(
        jnp.concatenate([attn_owned[:, q_cols : places[3]], attn_owned[:, places[4] : places[4] + 128]], axis=1),
        "tensor",
    )
    gain_owned = shared[:, 2 * head_dim :]
    return (
        output,
        tokens_grad,
        attn_owned[:, :q_cols],
        shared[:, :head_dim],
        shared[:, head_dim : 2 * head_dim],
        attn_owned[:, places[3] : places[4]].T,
        gain_owned[:, 0],
        gain_owned[:small, 4],
        gain_owned[:small, 5],
        gain_owned[:, 1],
        ffn_owned[:, :hidden_units],
        ffn_owned[:, hidden_units : 2 * hidden_units],
        ffn_owned[:, 2 * hidden_units :].T,
        gain_owned[:, 2],
        gain_owned[:, 3],
    )


def solution(mesh):
    return jax.shard_map(
        per_device,
        mesh=mesh,
        in_specs=(
            P(("dp", "tensor"), None),
            P("dp", "tensor"),
            P("dp", None),
            P("dp", None),
            P("tensor", "dp"),
            P("dp"),
            P("dp"),
            P("dp"),
            P("dp"),
            P("dp", "tensor"),
            P("dp", "tensor"),
            P("tensor", "dp"),
            P("dp"),
            P("dp"),
            P(("dp", "tensor"), None),
        ),
        out_specs=(
            P(("dp", "tensor"), None),
            P(("dp", "tensor"), None),
            P("dp", "tensor"),
            P("dp", None),
            P("dp", None),
            P("tensor", "dp"),
            P("dp"),
            P("dp"),
            P("dp"),
            P("dp"),
            P("dp", "tensor"),
            P("dp", "tensor"),
            P("tensor", "dp"),
            P("dp"),
            P("dp"),
        ),
        check_vma=False,
    )
```

```python
import functools
import math

import jax
import jax.numpy as jnp
from jax import lax
from jax.experimental import pallas as pl
from jax.experimental.pallas import tpu as pltpu
from jax.sharding import PartitionSpec as P

EPS = 1e-06
MASKED = -1e30


def matmul(left, right):
    return jnp.dot(left, right, preferred_element_type=jnp.float32)


def times_transposed(left, right):
    return lax.dot_general(
        left, right, (((1,), (1,)), ((), ())), preferred_element_type=jnp.float32
    )


def transposed_times(left, right):
    return lax.dot_general(
        left, right, (((0,), (0,)), ((), ())), preferred_element_type=jnp.float32
    )


def norm_rows(value, gain):
    scale = lax.rsqrt(jnp.mean(value * value, axis=-1, keepdims=True) + EPS)
    unit = value * scale
    return (unit * gain, unit, scale)


def norm_back(grad, unit, scale, gain, axes):
    gain_grad = jnp.sum(grad * unit, axis=axes)
    inner = grad * gain
    return (scale * (inner - unit * jnp.mean(inner * unit, axis=-1, keepdims=True)), gain_grad)


def tables(length, width, inner=64):
    half = width // 2
    freqs = jnp.exp(jnp.arange(half, dtype=jnp.float32) * (-2.0 * math.log(1000000.0) / width))
    coarse = (jnp.arange(length // inner, dtype=jnp.float32) * inner)[:, None] * freqs
    fine = jnp.arange(inner, dtype=jnp.float32)[:, None] * freqs
    cos_a, sin_a = jnp.cos(coarse)[:, None], jnp.sin(coarse)[:, None]
    cos_b, sin_b = jnp.cos(fine)[None], jnp.sin(fine)[None]
    cosine = (cos_a * cos_b - sin_a * sin_b).reshape(length, half)
    sine = (sin_a * cos_b + cos_a * sin_b).reshape(length, half)
    return cosine, sine


def turn(value, cosine, sine):
    half = value.shape[-1] // 2
    first, second = value[:, :half], value[:, half:]
    return jnp.concatenate(
        [first * cosine - second * sine, second * cosine + first * sine], axis=-1
    )


def turn_back(grad, cosine, sine):
    half = grad.shape[-1] // 2
    first, second = grad[:, :half], grad[:, half:]
    return jnp.concatenate(
        [first * cosine + second * sine, second * cosine - first * sine], axis=-1
    )


def gelu_tanh(value):
    return jax.nn.gelu(value, approximate=True)


def orders(bits, streams, n):
    near = list(range(bits - 1))
    turned = near[n % max(1, bits - 1) :] + near[: n % max(1, bits - 1)]
    return turned + ([bits - 1] if bits else [])


def partners(size, bit):
    return [(i, i ^ (1 << bit)) for i in range(size)]


class Gather:
    def __init__(self, share, size, order):
        self.size, self.order, self.done = size, list(reversed(order)), []
        self.rows, self.held = share.shape[0], share

    def step(self):
        bit = self.order[len(self.done)]
        other = lax.ppermute(self.held, "dp", partners(self.size, bit))
        upper = (lax.axis_index("dp") >> bit) & 1 == 1
        axis = sum(1 for seen in self.done if seen > bit)
        self.held = jnp.stack(
            [jnp.where(upper, other, self.held), jnp.where(upper, self.held, other)], axis=axis
        )
        self.done.append(bit)

    def result(self):
        return self.held.reshape(self.size * self.rows, self.held.shape[-1])


class Reduce:
    def __init__(self, whole, size, order):
        self.size, self.order, self.done = size, order, []
        bits = len(order)
        self.left = list(reversed(range(bits)))
        self.held = whole.reshape((2,) * bits + (whole.shape[0] // size, whole.shape[1]))

    def step(self):
        bit = self.order[len(self.done)]
        axis = self.left.index(bit)
        own = (lax.axis_index("dp") >> bit) & 1
        keep = lax.dynamic_index_in_dim(self.held, own, axis, keepdims=False)
        give = lax.dynamic_index_in_dim(self.held, 1 - own, axis, keepdims=False)
        other = lax.ppermute(give.astype(jnp.bfloat16), "dp", partners(self.size, bit))
        self.held = keep + other.astype(jnp.float32)
        self.left.remove(bit)
        self.done.append(bit)


def advance(streams, beside):
    for stream in streams:
        stream.step()
    tied = lax.optimization_barrier((tuple(s.held for s in streams), beside))
    for stream, held in zip(streams, tied[0]):
        stream.held = held
    return tied[1]


BLOCK = 512
VMEM = 56 * 1024 * 1024


def allowed_keys(size):
    keys = lax.broadcasted_iota(jnp.int32, (size, size), 0)
    queries = lax.broadcasted_iota(jnp.int32, (size, size), 1)
    return queries >= keys


def attend_kernel(heads, width, factor, q_ref, k_ref, vt_ref, o_ref, lse_ref, acc, peak, total):
    block = q_ref.shape[0]
    number = pl.program_id(0)
    queries = [q_ref[:, h * width : (h + 1) * width] * jnp.bfloat16(factor) for h in range(heads)]

    def tile(j, first):
        start = pl.multiple_of(j * block, block)
        keys = k_ref[pl.ds(start, block), :]
        values = vt_ref[:, pl.ds(start, block)]
        for h in range(heads):
            scores = times_transposed(keys, queries[h])
            if first:
                scores = jnp.where(allowed_keys(block), scores, MASKED)
                top = jnp.max(scores, axis=0, keepdims=True)
                expon = jnp.exp(scores - top)
                total[h] = jnp.sum(expon, axis=0, keepdims=True)
                acc[h] = matmul(values, expon.astype(jnp.bfloat16))
            else:
                old = peak[h]
                top = jnp.maximum(old, jnp.max(scores, axis=0, keepdims=True))
                expon = jnp.exp(scores - top)
                scale = jnp.exp(old - top)
                total[h] = total[h] * scale + jnp.sum(expon, axis=0, keepdims=True)
                acc[h] = acc[h] * scale + matmul(values, expon.astype(jnp.bfloat16))
            peak[h] = top

    tile(number, True)

    @pl.loop(0, number)
    def _(j):
        tile(j, False)

    for h in range(heads):
        mixed = acc[h] * (1.0 / total[h])
        o_ref[:, h * width : (h + 1) * width] = mixed.T.astype(jnp.bfloat16)
        lse_ref[h] = peak[h] + jnp.log(total[h])


def attend(query, key, value_t, heads):
    length, width = key.shape
    block = min(BLOCK, length)
    return pl.pallas_call(
        functools.partial(attend_kernel, heads, width, width ** (-0.5)),
        grid=(length // block,),
        in_specs=[
            pl.BlockSpec((block, heads * width), lambda i: (i, 0)),
            pl.BlockSpec((length, width), lambda i: (0, 0)),
            pl.BlockSpec((width, length), lambda i: (0, 0)),
        ],
        out_specs=[
            pl.BlockSpec((block, heads * width), lambda i: (i, 0)),
            pl.BlockSpec((heads, 1, block), lambda i: (0, 0, i)),
        ],
        out_shape=[
            jax.ShapeDtypeStruct((length, heads * width), jnp.bfloat16),
            jax.ShapeDtypeStruct((heads, 1, length), jnp.float32),
        ],
        scratch_shapes=[
            pltpu.VMEM((heads, width, block), jnp.float32),
            pltpu.VMEM((heads, 1, block), jnp.float32),
            pltpu.VMEM((heads, 1, block), jnp.float32),
        ],
        compiler_params=pltpu.CompilerParams(vmem_limit_bytes=VMEM),
        cost_estimate=pl.CostEstimate(
            flops=4 * heads * length * length * width,
            bytes_accessed=8 * length * heads * width,
            transcendentals=heads * length * length,
        ),
        name="attend",
    )(query, key, value_t)


def attend_back_kernel(
    heads, width, factor, q_ref, g_ref, o_ref, lse_ref, k_ref, kt_ref, v_ref,
    dq_ref, dk_ref, dv_ref, dqt, delta,
):
    block = q_ref.shape[0]
    number = pl.program_id(0)
    cols = [slice(h * width, (h + 1) * width) for h in range(heads)]
    queries = [q_ref[:, c] * jnp.bfloat16(factor) for c in cols]

    @pl.when(number == 0)
    def _():
        dk_ref[...] = jnp.zeros_like(dk_ref)
        dv_ref[...] = jnp.zeros_like(dv_ref)

    for h in range(heads):
        product = g_ref[:, cols[h]].astype(jnp.float32) * o_ref[:, cols[h]].astype(jnp.float32)
        delta[h] = jnp.sum(product.T, axis=0, keepdims=True)

    def tile(j, first):
        start = pl.multiple_of(j * block, block)
        rows = pl.ds(start, block)
        keys = k_ref[rows, :]
        keys_t = kt_ref[:, rows]
        values = v_ref[rows, :]
        key_grad = value_grad = None
        for h in range(heads):
            grads = g_ref[:, cols[h]]
            scores = times_transposed(keys, queries[h])
            prob = jnp.exp(scores - lse_ref[h])
            if first:
                prob = jnp.where(allowed_keys(block), prob, 0.0)
            prob_grad = times_transposed(values, grads)
            score_grad = (prob * (prob_grad - delta[h])).astype(jnp.bfloat16)
            more_value = matmul(prob.astype(jnp.bfloat16), grads)
            more_key = matmul(score_grad, queries[h])
            value_grad = more_value if value_grad is None else value_grad + more_value
            key_grad = more_key if key_grad is None else key_grad + more_key
            if first:
                dqt[h] = matmul(keys_t, score_grad)
            else:
                dqt[h] += matmul(keys_t, score_grad)
        dk_ref[rows, :] += key_grad
        dv_ref[rows, :] += value_grad

    tile(number, True)

    @pl.loop(0, number)
    def _(j):
        tile(j, False)

    for h in range(heads):
        dq_ref[:, cols[h]] = dqt[h].T * factor


def attend_back(query, grad, mixed, lse, key, key_t, value, heads):
    length, width = key.shape
    block = min(BLOCK, length)
    rows = pl.BlockSpec((block, heads * width), lambda i: (i, 0))
    whole = pl.BlockSpec((length, width), lambda i: (0, 0))
    return pl.pallas_call(
        functools.partial(attend_back_kernel, heads, width, width ** (-0.5)),
        grid=(length // block,),
        in_specs=[
            rows,
            rows,
            rows,
            pl.BlockSpec((heads, 1, block), lambda i: (0, 0, i)),
            whole,
            pl.BlockSpec((width, length), lambda i: (0, 0)),
            whole,
        ],
        out_specs=[rows, whole, whole],
        out_shape=[
            jax.ShapeDtypeStruct((length, heads * width), jnp.float32),
            jax.ShapeDtypeStruct((length, width), jnp.float32),
            jax.ShapeDtypeStruct((length, width), jnp.float32),
        ],
        scratch_shapes=[
            pltpu.VMEM((heads, width, block), jnp.float32),
            pltpu.VMEM((heads, 1, block), jnp.float32),
        ],
        compiler_params=pltpu.CompilerParams(vmem_limit_bytes=VMEM),
        cost_estimate=pl.CostEstimate(
            flops=10 * heads * length * length * width,
            bytes_accessed=12 * length * heads * width,
            transcendentals=heads * length * length,
        ),
        name="attend_back",
    )(query, grad, mixed, lse, key, key_t, value)


def per_device(
    tokens,
    w_query,
    w_key,
    w_value,
    w_out,
    gain_attn,
    gain_query,
    gain_key,
    gain_post_attn,
    w_gate,
    w_up,
    w_down,
    gain_pre_ffn,
    gain_post_ffn,
    cotangent,
):
    parts = lax.axis_size("tensor")
    spread = lax.axis_size("dp")
    own_rows = tokens.shape[0]
    length = own_rows * parts
    head_dim = w_key.shape[1]
    model = w_query.shape[0] * spread
    share = w_query.shape[0]
    small = gain_query.shape[0]
    heads = w_query.shape[1] // head_dim
    offset = lax.axis_index("tensor") * own_rows
    swap = [(i, (i + 1) % parts) for i in range(parts)]

    def whole_sequence(rows):
        pieces = [rows]
        for _ in range(parts - 1):
            pieces.append(lax.ppermute(pieces[-1], "tensor", swap))
        if parts == 1:
            return rows
        first = lax.axis_index("tensor") == 0
        return jnp.concatenate(
            [jnp.where(first, pieces[0], pieces[1]), jnp.where(first, pieces[1], pieces[0])], axis=0
        )

    def summed(partial):
        low = partial.astype(jnp.bfloat16)
        return low.astype(jnp.float32) + lax.ppermute(low, "tensor", swap).astype(jnp.float32)

    def own(rows):
        return lax.dynamic_slice_in_dim(rows, offset, own_rows, 0)

    def tall(column):
        return jnp.pad(column, (0, share - small))

    gain_block = jnp.stack(
        [gain_attn, gain_post_attn, gain_pre_ffn, gain_post_ffn, tall(gain_query), tall(gain_key)],
        axis=1,
    )
    gain_block = jnp.pad(gain_block, ((0, 0), (0, 128 - gain_block.shape[1])))
    bits = spread.bit_length() - 1
    assert spread == 1 << bits
    attn_streams = [
        Gather(share_of, spread, orders(bits, 3, n))
        for n, share_of in enumerate(
            [w_query, w_out.T, jnp.concatenate([w_key, w_value, gain_block], axis=1)]
        )
    ]
    for _ in range(bits):
        for stream in attn_streams:
            stream.step()
    query_w, out_wt, rest = (stream.result() for stream in attn_streams)
    (query_w, out_wt, rest), ffn_shares = lax.optimization_barrier(
        ((query_w, out_wt, rest), (w_gate, w_up, w_down.T))
    )
    ffn_streams = [
        Gather(share_of, spread, orders(bits, 3, n)) for n, share_of in enumerate(ffn_shares)
    ]
    low_tokens = whole_sequence(tokens)
    inputs = low_tokens.astype(jnp.float32)
    out_grad = whole_sequence(cotangent).astype(jnp.float32)

    q_cols = heads * head_dim
    key_w, value_w = rest[:, :head_dim], rest[:, head_dim : 2 * head_dim]
    gains = rest[:, 2 * head_dim :].astype(jnp.float32)
    attn_g, post_attn_g, pre_ffn_g, post_ffn_g = (gains[:, n] for n in range(4))
    query_g, key_g = (
        gains[:, n].reshape(spread, share)[:, :small].reshape(spread * small) for n in (4, 5)
    )
    cosine, sine = tables(length, head_dim)

    normed, attn_unit, attn_scale = norm_rows(inputs, attn_g)
    normed_low = normed.astype(jnp.bfloat16)
    for _ in range(bits - 3):
        normed_low = advance(ffn_streams, normed_low)
    key_pre = matmul(normed_low, key_w)
    value_low = matmul(normed_low, value_w).astype(jnp.bfloat16)
    key_normed, key_unit, key_scale = norm_rows(key_pre, key_g)
    key_low = turn(key_normed, cosine, sine).astype(jnp.bfloat16)
    query_pre = matmul(normed_low, query_w)
    if bits >= 3:
        query_pre = advance(ffn_streams, query_pre)
    query_units, query_scales, query_lows = [], [], []
    for h in range(heads):
        normal, unit, scale = norm_rows(query_pre[:, h * head_dim : (h + 1) * head_dim], query_g)
        query_units.append(unit)
        query_scales.append(scale)
        query_lows.append(turn(normal, cosine, sine).astype(jnp.bfloat16))
    query_low = jnp.concatenate(query_lows, axis=1)
    if bits >= 2:
        query_low = advance(ffn_streams, query_low)
    mixed, lse = attend(query_low, key_low, value_low.T, heads)
    if bits >= 1:
        mixed = advance(ffn_streams, mixed)
    gate_w, up_w, down_wt = (stream.result() for stream in ffn_streams)

    attn_sum = summed(times_transposed(mixed, out_wt))
    attn_branch, post_attn_unit, post_attn_scale = norm_rows(attn_sum, post_attn_g)
    middle = inputs + attn_branch
    ffn_normed, pre_ffn_unit, pre_ffn_scale = norm_rows(middle, pre_ffn_g)
    ffn_low = ffn_normed.astype(jnp.bfloat16)
    gate = matmul(ffn_low, gate_w)
    up = matmul(ffn_low, up_w)
    activated, gelu_pull = jax.vjp(gelu_tanh, gate)
    hidden = (activated * up).astype(jnp.bfloat16)
    ffn_sum = summed(times_transposed(hidden, down_wt))
    ffn_branch, post_ffn_unit, post_ffn_scale = norm_rows(ffn_sum, post_ffn_g)
    output = own((middle + ffn_branch).astype(jnp.bfloat16))

    ffn_sum_grad, post_ffn_gain_grad = norm_back(
        out_grad, post_ffn_unit, post_ffn_scale, post_ffn_g, 0
    )
    ffn_sum_low = ffn_sum_grad.astype(jnp.bfloat16)
    hidden_grad = matmul(ffn_sum_low, down_wt)
    gate_grad = gelu_pull(hidden_grad * up)[0].astype(jnp.bfloat16)
    up_grad = (hidden_grad * activated).astype(jnp.bfloat16)
    ffn_in_part = times_transposed(gate_grad, gate_w) + times_transposed(up_grad, up_w)
    ffn_in_grad = summed(ffn_in_part)
    ffn_grads = (
        transposed_times(ffn_low, gate_grad),
        transposed_times(ffn_low, up_grad),
        transposed_times(ffn_sum_low, hidden),
    )
    middle_part, pre_ffn_gain_grad = norm_back(
        ffn_in_grad, pre_ffn_unit, pre_ffn_scale, pre_ffn_g, 0
    )
    middle_grad = out_grad + middle_part
    attn_sum_grad, post_attn_gain_grad = norm_back(
        middle_grad, post_attn_unit, post_attn_scale, post_attn_g, 0
    )
    attn_sum_low = attn_sum_grad.astype(jnp.bfloat16)
    ffn_grads, attn_sum_low = lax.optimization_barrier((ffn_grads, attn_sum_low))
    ffn_sums = [
        Reduce(grads, spread, orders(bits, 3, n)) for n, grads in enumerate(ffn_grads)
    ]

    mixed_grad = matmul(attn_sum_low, out_wt).astype(jnp.bfloat16)
    out_wt_grad = transposed_times(attn_sum_low, mixed)
    query_grad, key_grad, value_grad = attend_back(
        query_low, mixed_grad, mixed, lse, key_low, key_low.T, value_low, heads
    )
    if bits >= 1:
        query_grad, key_grad = advance(ffn_sums, (query_grad, key_grad))
    query_gain_grad = 0.0
    query_pre_grads = []
    for h in range(heads):
        turned = turn_back(query_grad[:, h * head_dim : (h + 1) * head_dim], cosine, sine)
        pre_grad, gain_grad = norm_back(turned, query_units[h], query_scales[h], query_g, 0)
        query_pre_grads.append(pre_grad.astype(jnp.bfloat16))
        query_gain_grad = query_gain_grad + gain_grad
    if bits >= 2:
        query_pre_grads = advance(ffn_sums, query_pre_grads)
    key_turned = turn_back(key_grad, cosine, sine)
    key_pre_grad, key_gain_grad = norm_back(key_turned, key_unit, key_scale, key_g, 0)
    joint_grad = jnp.concatenate(
        query_pre_grads + [key_pre_grad.astype(jnp.bfloat16), value_grad.astype(jnp.bfloat16)],
        axis=1,
    )
    normed_part = (
        times_transposed(joint_grad[:, :q_cols], query_w)
        + times_transposed(joint_grad[:, q_cols : q_cols + head_dim], key_w)
        + times_transposed(joint_grad[:, q_cols + head_dim :], value_w)
    )
    query_w_grad = transposed_times(normed_low, joint_grad[:, :q_cols])
    other_w_grad = transposed_times(normed_low, joint_grad[:, q_cols:])
    for _ in range(bits - 2):
        query_w_grad, other_w_grad = advance(ffn_sums, (query_w_grad, other_w_grad))
    attn_gain_grad = jnp.sum(normed_part * attn_unit, axis=0)

    def wide(column):
        return jnp.pad(column.reshape(spread, small), ((0, 0), (0, share - small))).reshape(model)

    once = 1.0 / parts
    gain_grads = jnp.stack(
        [
            attn_gain_grad,
            post_attn_gain_grad * once,
            pre_ffn_gain_grad * once,
            post_ffn_gain_grad * once,
            wide(query_gain_grad),
            wide(key_gain_grad),
        ],
        axis=1,
    )
    gain_grads = jnp.pad(gain_grads, ((0, 0), (0, 128 - gain_grads.shape[1])))
    attn_sums = [
        Reduce(grads, spread, orders(bits, 3, n))
        for n, grads in enumerate(
            [query_w_grad, out_wt_grad, jnp.concatenate([other_w_grad, gain_grads], axis=1)]
        )
    ]
    for _ in range(bits):
        for stream in attn_sums:
            stream.step()
    query_owned, out_owned, shared = (stream.held for stream in attn_sums)
    normed_low_part = normed_part.astype(jnp.bfloat16)
    theirs = lax.dynamic_slice_in_dim(
        normed_low_part, (length - own_rows) - offset, own_rows, 0
    )
    normed_grad = own(normed_part) + lax.ppermute(theirs, "tensor", swap).astype(jnp.float32)
    input_part, _ = norm_back(normed_grad, own(attn_unit), own(attn_scale), attn_g, 0)
    tokens_grad = own(middle_grad) + input_part

    for _ in range(parts - 1):
        shared = shared + lax.ppermute(shared, "tensor", swap)
    gain_owned = shared[:, 2 * head_dim :]
    return (
        output,
        tokens_grad,
        query_owned,
        shared[:, :head_dim],
        shared[:, head_dim : 2 * head_dim],
        out_owned.T,
        gain_owned[:, 0],
        gain_owned[:small, 4],
        gain_owned[:small, 5],
        gain_owned[:, 1],
        ffn_sums[0].held,
        ffn_sums[1].held,
        ffn_sums[2].held.T,
        gain_owned[:, 2],
        gain_owned[:, 3],
    )


def solution(mesh):
    return jax.shard_map(
        per_device,
        mesh=mesh,
        in_specs=(
            P(("dp", "tensor"), None),
            P("dp", "tensor"),
            P("dp", None),
            P("dp", None),
            P("tensor", "dp"),
            P("dp"),
            P("dp"),
            P("dp"),
            P("dp"),
            P("dp", "tensor"),
            P("dp", "tensor"),
            P("tensor", "dp"),
            P("dp"),
            P("dp"),
            P(("dp", "tensor"), None),
        ),
        out_specs=(
            P(("dp", "tensor"), None),
            P(("dp", "tensor"), None),
            P("dp", "tensor"),
            P("dp", None),
            P("dp", None),
            P("tensor", "dp"),
            P("dp"),
            P("dp"),
            P("dp"),
            P("dp"),
            P("dp", "tensor"),
            P("dp", "tensor"),
            P("tensor", "dp"),
            P("dp"),
            P("dp"),
        ),
        check_vma=False,
    )
```

```python
import functools
import math

import jax
import jax.numpy as jnp
from jax import lax
from jax.experimental import pallas as pl
from jax.experimental.pallas import tpu as pltpu
from jax.sharding import PartitionSpec as P

EPS = 1e-06
MASKED = -1e30


def matmul(left, right):
    return jnp.dot(left, right, preferred_element_type=jnp.float32)


def times_transposed(left, right):
    return lax.dot_general(
        left, right, (((1,), (1,)), ((), ())), preferred_element_type=jnp.float32
    )


def transposed_times(left, right):
    return lax.dot_general(
        left, right, (((0,), (0,)), ((), ())), preferred_element_type=jnp.float32
    )


def norm_rows(value, gain):
    scale = lax.rsqrt(jnp.mean(value * value, axis=-1, keepdims=True) + EPS)
    unit = value * scale
    return (unit * gain, unit, scale)


def norm_back(grad, unit, scale, gain, axes):
    gain_grad = jnp.sum(grad * unit, axis=axes)
    inner = grad * gain
    return (scale * (inner - unit * jnp.mean(inner * unit, axis=-1, keepdims=True)), gain_grad)


def tables(length, width, inner=64):
    half = width // 2
    freqs = jnp.exp(jnp.arange(half, dtype=jnp.float32) * (-2.0 * math.log(1000000.0) / width))
    coarse = (jnp.arange(length // inner, dtype=jnp.float32) * inner)[:, None] * freqs
    fine = jnp.arange(inner, dtype=jnp.float32)[:, None] * freqs
    cos_a, sin_a = jnp.cos(coarse)[:, None], jnp.sin(coarse)[:, None]
    cos_b, sin_b = jnp.cos(fine)[None], jnp.sin(fine)[None]
    cosine = (cos_a * cos_b - sin_a * sin_b).reshape(length, half)
    sine = (sin_a * cos_b + cos_a * sin_b).reshape(length, half)
    return cosine, sine


def turn(value, cosine, sine):
    half = value.shape[-1] // 2
    first, second = value[:, :half], value[:, half:]
    return jnp.concatenate(
        [first * cosine - second * sine, second * cosine + first * sine], axis=-1
    )


def turn_back(grad, cosine, sine):
    half = grad.shape[-1] // 2
    first, second = grad[:, :half], grad[:, half:]
    return jnp.concatenate(
        [first * cosine + second * sine, second * cosine - first * sine], axis=-1
    )


def gelu_tanh(value):
    return jax.nn.gelu(value, approximate=True)


def orders(bits, streams, n):
    near = list(range(bits - 1))
    turned = near[n % max(1, bits - 1) :] + near[: n % max(1, bits - 1)]
    return turned + ([bits - 1] if bits else [])


def partners(size, bit):
    return [(i, i ^ (1 << bit)) for i in range(size)]


class Gather:
    def __init__(self, share, size, order):
        self.size, self.order, self.done = size, list(reversed(order)), []
        self.rows, self.held = share.shape[0], share

    def step(self):
        bit = self.order[len(self.done)]
        other = lax.ppermute(self.held, "dp", partners(self.size, bit))
        upper = (lax.axis_index("dp") >> bit) & 1 == 1
        axis = sum(1 for seen in self.done if seen > bit)
        self.held = jnp.stack(
            [jnp.where(upper, other, self.held), jnp.where(upper, self.held, other)], axis=axis
        )
        self.done.append(bit)

    def result(self):
        return self.held.reshape(self.size * self.rows, self.held.shape[-1])


class Reduce:
    def __init__(self, whole, size, order):
        self.size, self.order, self.done = size, order, []
        bits = len(order)
        self.left = list(reversed(range(bits)))
        self.held = whole.reshape((2,) * bits + (whole.shape[0] // size, whole.shape[1]))

    def step(self):
        bit = self.order[len(self.done)]
        axis = self.left.index(bit)
        own = (lax.axis_index("dp") >> bit) & 1
        keep = lax.dynamic_index_in_dim(self.held, own, axis, keepdims=False)
        give = lax.dynamic_index_in_dim(self.held, 1 - own, axis, keepdims=False)
        other = lax.ppermute(give.astype(jnp.bfloat16), "dp", partners(self.size, bit))
        self.held = keep + other.astype(jnp.float32)
        self.left.remove(bit)
        self.done.append(bit)


def advance(streams, beside):
    for stream in streams:
        stream.step()
    tied = lax.optimization_barrier((tuple(s.held for s in streams), beside))
    for stream, held in zip(streams, tied[0]):
        stream.held = held
    return tied[1]


def unfinished(streams):
    return [stream for stream in streams if stream.left]


BLOCK = 512
VMEM = 56 * 1024 * 1024


def allowed_keys(size):
    keys = lax.broadcasted_iota(jnp.int32, (size, size), 0)
    queries = lax.broadcasted_iota(jnp.int32, (size, size), 1)
    return queries >= keys


def attend_kernel(heads, width, factor, q_ref, k_ref, vt_ref, o_ref, lse_ref, acc, peak, total):
    block = q_ref.shape[0]
    number = pl.program_id(0)
    queries = [q_ref[:, h * width : (h + 1) * width] * jnp.bfloat16(factor) for h in range(heads)]

    def tile(j, first):
        start = pl.multiple_of(j * block, block)
        keys = k_ref[pl.ds(start, block), :]
        values = vt_ref[:, pl.ds(start, block)]
        for h in range(heads):
            scores = times_transposed(keys, queries[h])
            if first:
                scores = jnp.where(allowed_keys(block), scores, MASKED)
                top = jnp.max(scores, axis=0, keepdims=True)
                expon = jnp.exp(scores - top)
                total[h] = jnp.sum(expon, axis=0, keepdims=True)
                acc[h] = matmul(values, expon.astype(jnp.bfloat16))
            else:
                old = peak[h]
                top = jnp.maximum(old, jnp.max(scores, axis=0, keepdims=True))
                expon = jnp.exp(scores - top)
                scale = jnp.exp(old - top)
                total[h] = total[h] * scale + jnp.sum(expon, axis=0, keepdims=True)
                acc[h] = acc[h] * scale + matmul(values, expon.astype(jnp.bfloat16))
            peak[h] = top

    tile(number, True)

    @pl.loop(0, number)
    def _(j):
        tile(j, False)

    for h in range(heads):
        mixed = acc[h] * (1.0 / total[h])
        o_ref[:, h * width : (h + 1) * width] = mixed.T.astype(jnp.bfloat16)
        lse_ref[h] = peak[h] + jnp.log(total[h])


def attend(query, key, value_t, heads):
    length, width = key.shape
    block = min(BLOCK, length)
    return pl.pallas_call(
        functools.partial(attend_kernel, heads, width, width ** (-0.5)),
        grid=(length // block,),
        in_specs=[
            pl.BlockSpec((block, heads * width), lambda i: (i, 0)),
            pl.BlockSpec((length, width), lambda i: (0, 0)),
            pl.BlockSpec((width, length), lambda i: (0, 0)),
        ],
        out_specs=[
            pl.BlockSpec((block, heads * width), lambda i: (i, 0)),
            pl.BlockSpec((heads, 1, block), lambda i: (0, 0, i)),
        ],
        out_shape=[
            jax.ShapeDtypeStruct((length, heads * width), jnp.bfloat16),
            jax.ShapeDtypeStruct((heads, 1, length), jnp.float32),
        ],
        scratch_shapes=[
            pltpu.VMEM((heads, width, block), jnp.float32),
            pltpu.VMEM((heads, 1, block), jnp.float32),
            pltpu.VMEM((heads, 1, block), jnp.float32),
        ],
        compiler_params=pltpu.CompilerParams(vmem_limit_bytes=VMEM),
        cost_estimate=pl.CostEstimate(
            flops=4 * heads * length * length * width,
            bytes_accessed=8 * length * heads * width,
            transcendentals=heads * length * length,
        ),
        name="attend",
    )(query, key, value_t)


def attend_back_kernel(
    heads, width, factor, q_ref, g_ref, o_ref, lse_ref, k_ref, kt_ref, v_ref,
    dq_ref, dk_ref, dv_ref, dqt, delta,
):
    block = q_ref.shape[0]
    number = pl.program_id(0)
    cols = [slice(h * width, (h + 1) * width) for h in range(heads)]
    queries = [q_ref[:, c] * jnp.bfloat16(factor) for c in cols]

    @pl.when(number == 0)
    def _():
        dk_ref[...] = jnp.zeros_like(dk_ref)
        dv_ref[...] = jnp.zeros_like(dv_ref)

    for h in range(heads):
        product = g_ref[:, cols[h]].astype(jnp.float32) * o_ref[:, cols[h]].astype(jnp.float32)
        delta[h] = jnp.sum(product.T, axis=0, keepdims=True)

    def tile(j, first):
        start = pl.multiple_of(j * block, block)
        rows = pl.ds(start, block)
        keys = k_ref[rows, :]
        keys_t = kt_ref[:, rows]
        values = v_ref[rows, :]
        key_grad = value_grad = None
        for h in range(heads):
            grads = g_ref[:, cols[h]]
            scores = times_transposed(keys, queries[h])
            prob = jnp.exp(scores - lse_ref[h])
            if first:
                prob = jnp.where(allowed_keys(block), prob, 0.0)
            prob_grad = times_transposed(values, grads)
            score_grad = (prob * (prob_grad - delta[h])).astype(jnp.bfloat16)
            more_value = matmul(prob.astype(jnp.bfloat16), grads)
            more_key = matmul(score_grad, queries[h])
            value_grad = more_value if value_grad is None else value_grad + more_value
            key_grad = more_key if key_grad is None else key_grad + more_key
            if first:
                dqt[h] = matmul(keys_t, score_grad)
            else:
                dqt[h] += matmul(keys_t, score_grad)
        dk_ref[rows, :] += key_grad
        dv_ref[rows, :] += value_grad

    tile(number, True)

    @pl.loop(0, number)
    def _(j):
        tile(j, False)

    for h in range(heads):
        dq_ref[:, cols[h]] = dqt[h].T * factor


def attend_back(query, grad, mixed, lse, key, key_t, value, heads):
    length, width = key.shape
    block = min(BLOCK, length)
    rows = pl.BlockSpec((block, heads * width), lambda i: (i, 0))
    whole = pl.BlockSpec((length, width), lambda i: (0, 0))
    return pl.pallas_call(
        functools.partial(attend_back_kernel, heads, width, width ** (-0.5)),
        grid=(length // block,),
        in_specs=[
            rows,
            rows,
            rows,
            pl.BlockSpec((heads, 1, block), lambda i: (0, 0, i)),
            whole,
            pl.BlockSpec((width, length), lambda i: (0, 0)),
            whole,
        ],
        out_specs=[rows, whole, whole],
        out_shape=[
            jax.ShapeDtypeStruct((length, heads * width), jnp.float32),
            jax.ShapeDtypeStruct((length, width), jnp.float32),
            jax.ShapeDtypeStruct((length, width), jnp.float32),
        ],
        scratch_shapes=[
            pltpu.VMEM((heads, width, block), jnp.float32),
            pltpu.VMEM((heads, 1, block), jnp.float32),
        ],
        compiler_params=pltpu.CompilerParams(vmem_limit_bytes=VMEM),
        cost_estimate=pl.CostEstimate(
            flops=10 * heads * length * length * width,
            bytes_accessed=12 * length * heads * width,
            transcendentals=heads * length * length,
        ),
        name="attend_back",
    )(query, grad, mixed, lse, key, key_t, value)


def per_device(
    tokens,
    w_query,
    w_key,
    w_value,
    w_out,
    gain_attn,
    gain_query,
    gain_key,
    gain_post_attn,
    w_gate,
    w_up,
    w_down,
    gain_pre_ffn,
    gain_post_ffn,
    cotangent,
):
    parts = lax.axis_size("tensor")
    spread = lax.axis_size("dp")
    own_rows = tokens.shape[0]
    length = own_rows * parts
    head_dim = w_key.shape[1]
    model = w_query.shape[0] * spread
    share = w_query.shape[0]
    small = gain_query.shape[0]
    heads = w_query.shape[1] // head_dim
    offset = lax.axis_index("tensor") * own_rows
    swap = [(i, (i + 1) % parts) for i in range(parts)]

    def whole_sequence(rows):
        pieces = [rows]
        for _ in range(parts - 1):
            pieces.append(lax.ppermute(pieces[-1], "tensor", swap))
        if parts == 1:
            return rows
        first = lax.axis_index("tensor") == 0
        return jnp.concatenate(
            [jnp.where(first, pieces[0], pieces[1]), jnp.where(first, pieces[1], pieces[0])], axis=0
        )

    def summed(partial):
        low = partial.astype(jnp.bfloat16)
        return low.astype(jnp.float32) + lax.ppermute(low, "tensor", swap).astype(jnp.float32)

    def own(rows):
        return lax.dynamic_slice_in_dim(rows, offset, own_rows, 0)

    def tall(column):
        return jnp.pad(column, (0, share - small))

    gain_block = jnp.stack(
        [gain_attn, gain_post_attn, gain_pre_ffn, gain_post_ffn, tall(gain_query), tall(gain_key)],
        axis=1,
    )
    gain_block = jnp.pad(gain_block, ((0, 0), (0, 128 - gain_block.shape[1])))
    bits = spread.bit_length() - 1
    assert spread == 1 << bits
    attn_streams = [
        Gather(share_of, spread, orders(bits, 3, n))
        for n, share_of in enumerate(
            [w_query, w_out.T, jnp.concatenate([w_key, w_value, gain_block], axis=1)]
        )
    ]
    for _ in range(bits):
        for stream in attn_streams:
            stream.step()
    query_w, out_wt, rest = (stream.result() for stream in attn_streams)
    (query_w, out_wt, rest), ffn_shares = lax.optimization_barrier(
        ((query_w, out_wt, rest), (w_gate, w_up, w_down.T))
    )
    ffn_streams = [
        Gather(share_of, spread, orders(bits, 3, n)) for n, share_of in enumerate(ffn_shares)
    ]
    low_tokens = whole_sequence(tokens)
    inputs = low_tokens.astype(jnp.float32)
    out_grad = whole_sequence(cotangent).astype(jnp.float32)

    q_cols = heads * head_dim
    key_w, value_w = rest[:, :head_dim], rest[:, head_dim : 2 * head_dim]
    gains = rest[:, 2 * head_dim :].astype(jnp.float32)
    attn_g, post_attn_g, pre_ffn_g, post_ffn_g = (gains[:, n] for n in range(4))
    query_g, key_g = (
        gains[:, n].reshape(spread, share)[:, :small].reshape(spread * small) for n in (4, 5)
    )
    cosine, sine = tables(length, head_dim)

    normed, attn_unit, attn_scale = norm_rows(inputs, attn_g)
    normed_low = normed.astype(jnp.bfloat16)
    for _ in range(bits - 3):
        normed_low = advance(ffn_streams, normed_low)
    key_pre = matmul(normed_low, key_w)
    value_low = matmul(normed_low, value_w).astype(jnp.bfloat16)
    key_normed, key_unit, key_scale = norm_rows(key_pre, key_g)
    key_low = turn(key_normed, cosine, sine).astype(jnp.bfloat16)
    query_pre = matmul(normed_low, query_w)
    if bits >= 3:
        query_pre = advance(ffn_streams, query_pre)
    query_units, query_scales, query_lows = [], [], []
    for h in range(heads):
        normal, unit, scale = norm_rows(query_pre[:, h * head_dim : (h + 1) * head_dim], query_g)
        query_units.append(unit)
        query_scales.append(scale)
        query_lows.append(turn(normal, cosine, sine).astype(jnp.bfloat16))
    query_low = jnp.concatenate(query_lows, axis=1)
    if bits >= 2:
        query_low = advance(ffn_streams, query_low)
    mixed, lse = attend(query_low, key_low, value_low.T, heads)
    if bits >= 1:
        mixed = advance(ffn_streams, mixed)
    gate_w, up_w, down_wt = (stream.result() for stream in ffn_streams)

    attn_sum = summed(times_transposed(mixed, out_wt))
    attn_branch, post_attn_unit, post_attn_scale = norm_rows(attn_sum, post_attn_g)
    middle = inputs + attn_branch
    ffn_normed, pre_ffn_unit, pre_ffn_scale = norm_rows(middle, pre_ffn_g)
    ffn_low = ffn_normed.astype(jnp.bfloat16)
    gate = matmul(ffn_low, gate_w)
    up = matmul(ffn_low, up_w)
    activated, gelu_pull = jax.vjp(gelu_tanh, gate)
    hidden = (activated * up).astype(jnp.bfloat16)
    ffn_sum = summed(times_transposed(hidden, down_wt))
    ffn_branch, post_ffn_unit, post_ffn_scale = norm_rows(ffn_sum, post_ffn_g)
    output = own((middle + ffn_branch).astype(jnp.bfloat16))

    ffn_sum_grad, post_ffn_gain_grad = norm_back(
        out_grad, post_ffn_unit, post_ffn_scale, post_ffn_g, 0
    )
    ffn_sum_low = ffn_sum_grad.astype(jnp.bfloat16)
    hidden_grad = matmul(ffn_sum_low, down_wt)
    gate_grad = gelu_pull(hidden_grad * up)[0].astype(jnp.bfloat16)
    up_grad = (hidden_grad * activated).astype(jnp.bfloat16)
    ffn_in_part = times_transposed(gate_grad, gate_w) + times_transposed(up_grad, up_w)
    ffn_in_grad = summed(ffn_in_part)
    ffn_grads = (
        transposed_times(ffn_low, gate_grad),
        transposed_times(ffn_low, up_grad),
        transposed_times(ffn_sum_low, hidden),
    )
    middle_part, pre_ffn_gain_grad = norm_back(
        ffn_in_grad, pre_ffn_unit, pre_ffn_scale, pre_ffn_g, 0
    )
    middle_grad = out_grad + middle_part
    attn_sum_grad, post_attn_gain_grad = norm_back(
        middle_grad, post_attn_unit, post_attn_scale, post_attn_g, 0
    )
    attn_sum_low = attn_sum_grad.astype(jnp.bfloat16)
    ffn_grads, attn_sum_low = lax.optimization_barrier((ffn_grads, attn_sum_low))
    mixed_grad = matmul(attn_sum_low, out_wt).astype(jnp.bfloat16)
    out_wt_grad = transposed_times(attn_sum_low, mixed)
    early_sums = [
        Reduce(grads, spread, orders(bits, 3, n))
        for n, grads in enumerate(ffn_grads + (out_wt_grad,))
    ]
    query_grad, key_grad, value_grad = attend_back(
        query_low, mixed_grad, mixed, lse, key_low, key_low.T, value_low, heads
    )
    if bits >= 1:
        query_grad, key_grad = advance(early_sums, (query_grad, key_grad))
    query_gain_grad = 0.0
    query_pre_grads = []
    for h in range(heads):
        turned = turn_back(query_grad[:, h * head_dim : (h + 1) * head_dim], cosine, sine)
        pre_grad, gain_grad = norm_back(turned, query_units[h], query_scales[h], query_g, 0)
        query_pre_grads.append(pre_grad.astype(jnp.bfloat16))
        query_gain_grad = query_gain_grad + gain_grad
    if bits >= 2:
        query_pre_grads = advance(early_sums, query_pre_grads)
    key_turned = turn_back(key_grad, cosine, sine)
    key_pre_grad, key_gain_grad = norm_back(key_turned, key_unit, key_scale, key_g, 0)
    joint_grad = jnp.concatenate(
        query_pre_grads + [key_pre_grad.astype(jnp.bfloat16), value_grad.astype(jnp.bfloat16)],
        axis=1,
    )
    normed_part = (
        times_transposed(joint_grad[:, :q_cols], query_w)
        + times_transposed(joint_grad[:, q_cols : q_cols + head_dim], key_w)
        + times_transposed(joint_grad[:, q_cols + head_dim :], value_w)
    )
    query_w_grad = transposed_times(normed_low, joint_grad[:, :q_cols])
    other_w_grad = transposed_times(normed_low, joint_grad[:, q_cols:])
    attn_gain_grad = jnp.sum(normed_part * attn_unit, axis=0)
    query_sum = Reduce(query_w_grad, spread, orders(bits, 3, 1))
    sums = early_sums + [query_sum]
    normed_part, attn_gain_grad = advance(unfinished(sums), (normed_part, attn_gain_grad))

    def wide(column):
        return jnp.pad(column.reshape(spread, small), ((0, 0), (0, share - small))).reshape(model)

    once = 1.0 / parts
    gain_grads = jnp.stack(
        [
            attn_gain_grad,
            post_attn_gain_grad * once,
            pre_ffn_gain_grad * once,
            post_ffn_gain_grad * once,
            wide(query_gain_grad),
            wide(key_gain_grad),
        ],
        axis=1,
    )
    gain_grads = jnp.pad(gain_grads, ((0, 0), (0, 128 - gain_grads.shape[1])))
    other_sum = Reduce(
        jnp.concatenate([other_w_grad, gain_grads], axis=1), spread, orders(bits, 3, 2)
    )
    sums = sums + [other_sum]
    while unfinished(sums):
        advance(unfinished(sums), ())
    shared = other_sum.held
    normed_low_part = normed_part.astype(jnp.bfloat16)
    theirs = lax.dynamic_slice_in_dim(
        normed_low_part, (length - own_rows) - offset, own_rows, 0
    )
    normed_grad = own(normed_part) + lax.ppermute(theirs, "tensor", swap).astype(jnp.float32)
    input_part, _ = norm_back(normed_grad, own(attn_unit), own(attn_scale), attn_g, 0)
    tokens_grad = own(middle_grad) + input_part

    for _ in range(parts - 1):
        shared = shared + lax.ppermute(shared, "tensor", swap)
    gain_owned = shared[:, 2 * head_dim :]
    return (
        output,
        tokens_grad,
        query_sum.held,
        shared[:, :head_dim],
        shared[:, head_dim : 2 * head_dim],
        early_sums[3].held.T,
        gain_owned[:, 0],
        gain_owned[:small, 4],
        gain_owned[:small, 5],
        gain_owned[:, 1],
        early_sums[0].held,
        early_sums[1].held,
        early_sums[2].held.T,
        gain_owned[:, 2],
        gain_owned[:, 3],
    )


def solution(mesh):
    return jax.shard_map(
        per_device,
        mesh=mesh,
        in_specs=(
            P(("dp", "tensor"), None),
            P("dp", "tensor"),
            P("dp", None),
            P("dp", None),
            P("tensor", "dp"),
            P("dp"),
            P("dp"),
            P("dp"),
            P("dp"),
            P("dp", "tensor"),
            P("dp", "tensor"),
            P("tensor", "dp"),
            P("dp"),
            P("dp"),
            P(("dp", "tensor"), None),
        ),
        out_specs=(
            P(("dp", "tensor"), None),
            P(("dp", "tensor"), None),
            P("dp", "tensor"),
            P("dp", None),
            P("dp", None),
            P("tensor", "dp"),
            P("dp"),
            P("dp"),
            P("dp"),
            P("dp"),
            P("dp", "tensor"),
            P("dp", "tensor"),
            P("tensor", "dp"),
            P("dp"),
            P("dp"),
        ),
        check_vma=False,
    )
```
